512 devices in a mesh: gx: 32 (over x, z_hi, y), gy: 16 (over z_lo, core).
Axes of the slice: x: 4, y: 4, z: 16 (z_hi: 2, z_lo: 8; z = z_hi * 8 + z_lo), core: 2. Of those that a mesh axis runs over, the one named last changes fastest.
Arguments:
- start_vectors: bfloat16 [128, 32, 128, 128], P('gx', 'gy'), may hold values from -6 to 6
- blocks: bfloat16 [128, 32, 7, 128, 128], P('gx', 'gy'), as said below
- neighbour: int32 [128, 32, 7], P('gx', 'gy'), may hold values from 0 to 8, as said below
- counts: int32 [128, 32], P('gx', 'gy'), may hold values from 1 to 7, as said below
Outputs:
- moments: float32 [5, 128], replicated
- last_vector: bfloat16 [128, 32, 128, 128], P('gx', 'gy')
The draws below stay inside these ranges and needn't reach their ends.
Inputs may be any that keep to these rules, and one draw needn't show every extreme that they name: `neighbour`: each tile's 7 slots name the codes 0, 1, 3, 4, 5, 7, 8 once each, its live slots first; code 4 (the tile itself) is always live; tile t couples to tile t + d through a live slot exactly when tile t + d couples to t through a live slot of the opposite code. `counts`: one plus the number of the tile's live couplings to other tiles. The block of a live coupling of tile t + d back to tile t is the transpose of the block of tile t towards t + d; blocks of code 4 are symmetric.
All inputs are finite; a program needn't handle non-finite values.
Results may differ from the reference program's by a relative error of at most 0.0045.
Values may be sent and summed in bfloat16 or wider, within the bound.
A program may use at most 64 MiB of HBM per device.

```python
import math
import jax
import jax.numpy as jnp
from jax import lax

ORB = 128
NB = 7
R = 128
ITERS = 4
NTX = 128
NTY = 32
ROWS = 524288


def coupling_pattern(key):
    steps_x = [1, 0, 1]
    steps_y = [0, 1, 1]
    live_key = jax.random.fold_in(key, 101)
    rank_key = jax.random.fold_in(key, 102)
    bonds = (jax.random.randint(live_key, (NTX, NTY, 3), 0, 4, dtype=jnp.int32) < 3).astype(jnp.int32)
    row_pos = jnp.arange(NTX, dtype=jnp.int32)[:, None, None]
    col_pos = jnp.arange(NTY, dtype=jnp.int32)[None, :, None]
    move_x = jnp.array(steps_x, dtype=jnp.int32)[None, None, :]
    move_y = jnp.array(steps_y, dtype=jnp.int32)[None, None, :]
    empty_x = NTX // 2
    empty_y = NTY // 2
    at_anchor = (row_pos == 0) & (col_pos == 0) | (row_pos == (NTX - move_x) % NTX) & (col_pos == (NTY - move_y) % NTY)
    at_empty = (row_pos == empty_x) & (col_pos == empty_y) | (row_pos == empty_x - move_x) & (col_pos == empty_y - move_y)
    bonds = jnp.where(at_anchor, 1, jnp.where(at_empty, 0, bonds)).astype(jnp.int32)
    backward = jnp.stack([jnp.roll(bonds[:, :, which], (steps_x[which], steps_y[which]), axis=(0, 1)) for which in range(3)], axis=2)
    flags = jnp.concatenate([jnp.ones((NTX, NTY, 1), jnp.int32), bonds, backward], axis=2)
    scores = (1 - flags) * 64 + jax.random.randint(rank_key, (NTX, NTY, 7), 0, 8, dtype=jnp.int32) * 8 + jnp.arange(7, dtype=jnp.int32)[None, None, :]
    arrangement = jnp.argsort(scores, axis=2, stable=True).astype(jnp.int32)
    code_table = jnp.array([4, 7, 5, 8, 1, 3, 0], dtype=jnp.int32)
    codes = jnp.take(code_table, arrangement).astype(jnp.int32)
    live_count = (1 + jnp.sum(bonds, axis=2) + jnp.sum(backward, axis=2)).astype(jnp.int32)
    return (arrangement, codes, live_count)


def draw_neighbour(key, part):
    arrangement, codes, live_count = coupling_pattern(key)
    return codes


def draw_counts(key, part):
    arrangement, codes, live_count = coupling_pattern(key)
    return live_count


def draw_blocks(key, part):
    arrangement, codes, live_count = coupling_pattern(key)
    key = jax.random.fold_in(key, 7)
    steps_x = [1, 0, 1]
    steps_y = [0, 1, 1]
    spread = 0.25 / math.sqrt(NB * ORB)
    hopping = jax.random.normal(jax.random.fold_in(key, 1), (NTX, NTY, 3, ORB, ORB), jnp.float32) * spread
    onsite = jax.random.normal(jax.random.fold_in(key, 2), (NTX, NTY, ORB, ORB), jnp.float32) * spread
    onsite = (onsite + jnp.swapaxes(onsite, 2, 3)) * (1.0 / math.sqrt(2.0))
    angle_x = jnp.arange(NTX, dtype=jnp.float32) * (2.0 * math.pi / NTX)
    angle_y = jnp.arange(NTY, dtype=jnp.float32) * (2.0 * math.pi / NTY)
    moire = jnp.cos(angle_x)[:, None, None] * jnp.cos(angle_y)[None, :, None]
    rough = jax.random.uniform(jax.random.fold_in(key, 3), (NTX, NTY, ORB), jnp.float32, -1.0, 1.0)
    energy = 0.1 + 0.08 * moire + 0.12 * rough
    identity = jnp.eye(ORB, dtype=jnp.float32)[None, None, :, :]
    onsite = onsite + energy[:, :, :, None] * identity
    forward = [hopping[:, :, which] for which in range(3)]
    returning = [jnp.swapaxes(jnp.roll(hopping[:, :, which], (steps_x[which], steps_y[which]), axis=(0, 1)), 2, 3) for which in range(3)]
    every_kind = jnp.stack([onsite] + forward + returning, axis=2)
    chosen = jnp.take_along_axis(every_kind, arrangement[:, :, :, None, None], axis=2)
    return chosen.astype(jnp.bfloat16)


def shard_levels(key, shape, split, low, largest):
    def one(position, blocks):
        steps = jax.random.uniform(jax.random.fold_in(jax.random.fold_in(key, 6), position), (blocks,), jnp.float32, low / len(split), largest / len(split))
        return jnp.repeat(jnp.exp(steps), shape[position] // blocks).reshape((-1,) + (1,) * (len(shape) - position - 1))

    level = one(*split[0])
    for cut in split[1:]:
        level = level * one(*cut)
    return level


def normal_values(rng, shape, scale, most, pieces=(), kind=jnp.bfloat16):
    values = jax.random.normal(rng, shape, jnp.float32) * scale
    if len(pieces) > 0:
        values = shard_levels(rng, shape, pieces, -0.22, 0.18) * values
    return jnp.clip(values, min=-most, max=most).astype(kind)


def setup_inputs(seed: int = 0) -> dict:
    arg_keys = jax.random.split(jax.random.key(seed), 5)
    return {
        "start_vectors": normal_values(arg_keys[0], (NTX, NTY, R, ORB), 1.0, 6.0, ((0, 32), (1, 16))),
        "blocks": draw_blocks(jax.random.fold_in(arg_keys[4], 71), 0),
        "neighbour": draw_neighbour(jax.random.fold_in(arg_keys[4], 71), 0),
        "counts": draw_counts(jax.random.fold_in(arg_keys[4], 71), 0),
    }


def apply_operator(vec, blocks, neighbour, counts):
    flat = vec.reshape(NTX * NTY, R, ORB)
    xs = jnp.arange(NTX, dtype=jnp.int32)[:, None]
    ys = jnp.arange(NTY, dtype=jnp.int32)[None, :]

    def slot(acc, j):
        code = lax.dynamic_index_in_dim(neighbour, j, 2, keepdims=False)
        shift_x = code // 3 - 1
        shift_y = code % 3 - 1
        index = (((xs + shift_x) % NTX) * NTY + (ys + shift_y) % NTY).astype(jnp.int32)
        piece = flat[index].astype(jnp.float32)
        block = lax.dynamic_index_in_dim(blocks, j, 2, keepdims=False).astype(jnp.float32)
        product = jnp.einsum("xyrb,xyba->xyra", piece, block)
        live = (j < counts).astype(jnp.float32)[:, :, None, None]
        return acc + live * product, None

    start = jnp.zeros((NTX, NTY, R, ORB), jnp.float32)
    total, unused = lax.scan(slot, start, jnp.arange(NB, dtype=jnp.int32))
    return total


def reference(start_vectors, blocks, neighbour, counts):
    first = start_vectors.astype(jnp.float32)
    sums = [jnp.sum(first * first, axis=(0, 1, 3)) / ROWS]
    previous = first
    current = apply_operator(start_vectors, blocks, neighbour, counts)
    sums.append(jnp.sum(first * current, axis=(0, 1, 3)) / ROWS)
    for step in range(ITERS - 1):
        image = apply_operator(current.astype(jnp.bfloat16), blocks, neighbour, counts)
        following = 2.0 * image - previous
        previous, current = current, following
        sums.append(jnp.sum(first * current, axis=(0, 1, 3)) / ROWS)
    return jnp.stack(sums), current.astype(jnp.bfloat16)
```

```python
import functools

import jax
import jax.numpy as jnp
from jax import lax
from jax.experimental import pallas as pl
from jax.experimental.pallas import tpu as pltpu
from jax.sharding import PartitionSpec as P

ITERS = 4
GROUPS = 2
Y_SIZE = 4
Z_HALVES = 2
CORES = 2
MESH = pl.DeviceIdType.MESH


def kernel(
    gx_n, gy_n, groups, total_rows,
    start_ref, blocks_ref, code_ref, count_ref,
    moments_ref, last_ref,
    raw, wx, wy, b, v, acc, xh, yh, part, ga, gb, gc,
    load_sem, out_sem, send_sem, recv_sem, ga_sem, gb_send, gb_recv, gc_send, gc_recv,
):
    tiles_x, tiles_y, slots = code_ref.shape
    vectors, orb = start_ref.shape[2:]
    rows = vectors // groups
    pair = 2 * orb
    last = tiles_x - 1

    gx, gy = lax.axis_index("gx"), lax.axis_index("gy")
    east, west = lax.rem(gx + 1, gx_n), lax.rem(gx + gx_n - 1, gx_n)
    north, south = lax.rem(gy + 1, gy_n), lax.rem(gy + gy_n - 1, gy_n)

    x_size = gx_n // (Y_SIZE * Z_HALVES)
    z_lows = gy_n // CORES
    px = lax.div(gx, Y_SIZE * Z_HALVES)
    z_high = lax.rem(lax.div(gx, Y_SIZE), Z_HALVES)
    py = lax.rem(gx, Y_SIZE)
    z_low, core = lax.div(gy, CORES), lax.rem(gy, CORES)
    plane_n, line_n = x_size * Y_SIZE, Z_HALVES * z_lows
    my_plane, my_line = px * Y_SIZE + py, z_high * z_lows + z_low
    sibling = (gx, z_low * CORES + 1 - core)

    def plane_peer(p):
        peer_x, peer_y = lax.div(p, Y_SIZE), lax.rem(p, Y_SIZE)
        return (peer_x * (Y_SIZE * Z_HALVES) + z_high * Y_SIZE + peer_y, gy)

    def line_peer(p):
        high, low = lax.div(p, z_lows), lax.rem(p, z_lows)
        return (px * (Y_SIZE * Z_HALVES) + high * Y_SIZE + py, low * CORES + core)

    barrier = pltpu.get_barrier_semaphore()

    def greet(device):
        pl.semaphore_signal(barrier, inc=1, device_id=device, device_id_type=MESH)

    for device in (
        (east, gy), (west, gy), (east, north), (west, south), (gx, north), (gx, south), sibling,
    ):
        greet(device)

    @pl.loop(1, line_n)
    def _(j):
        greet(line_peer(lax.rem(my_line + j, line_n)))

    @pl.loop(1, plane_n)
    def _(j):
        greet(plane_peer(lax.rem(my_plane + j, plane_n)))

    load_start = pltpu.make_async_copy(start_ref, b.at[0], load_sem.at[0])
    load_blocks = pltpu.make_async_copy(
        blocks_ref, raw.at[:, :, pl.ds(0, slots)], load_sem.at[1]
    )
    load_blocks.start()
    load_start.start()

    def rows_of(g):
        return pl.ds(pl.multiple_of(g * rows, rows), rows)

    def messages(k, g):
        r = rows_of(g)
        ends = (
            (b.at[k, last, :, r], xh.at[k, 0, :, r], (east, gy)),
            (b.at[k, 0, :, r], xh.at[k, 1, :, r], (west, gy)),
            (b.at[k, last, 1, r], yh.at[k, 0, 0, r], (east, north)),
            (b.at[k, 0, 0, r], yh.at[k, 1, tiles_x, r], (west, south)),
            (b.at[k, :, 1, r], yh.at[k, 0, pl.ds(1, tiles_x), r], (gx, north)),
            (b.at[k, :, 0, r], yh.at[k, 1, pl.ds(0, tiles_x), r], (gx, south)),
        )
        return [
            pltpu.make_async_remote_copy(
                src_ref=source,
                dst_ref=target,
                send_sem=send_sem.at[k * groups + g, m],
                recv_sem=recv_sem.at[k * groups + g, m],
                device_id=device,
                device_id_type=MESH,
            )
            for m, (source, target, device) in enumerate(ends)
        ]

    def interior(k, g):
        r = rows_of(g)
        for x in range(tiles_x):
            low, high = max(x - 1, 0), min(x + 1, last)
            left = jnp.concatenate(
                [b[k, s, y, r, :] for s in range(low, high + 1) for y in range(2)], axis=1
            )
            right = wx[x, (low - x + 1) * pair : (high - x + 2) * pair, :]
            acc[g, x] = jnp.dot(left, right, preferred_element_type=jnp.float32)

    def rim(k, g, x, side):
        r = rows_of(g)
        left = jnp.concatenate([yh[k, side, x, r, :], yh[k, side, x + 1, r, :]], axis=1)
        return jnp.dot(left, wy[x, side], preferred_element_type=jnp.float32)

    def finish(k, g, x, image):
        r = rows_of(g)
        scale = jnp.where(k == 0, 1.0, 2.0)
        value = scale * image - v[k, x, r, :]
        v[k + 2, x, r, :] = value
        rounded = value.astype(jnp.bfloat16)
        for y in range(2):
            b[k + 1, x, y, r, :] = rounded[:, y * orb : (y + 1) * orb]

    load_start.wait()
    v[0] = jnp.zeros(v.shape[1:], v.dtype)
    for x in range(tiles_x):
        for y in range(2):
            v[1, x, :, y * orb : (y + 1) * orb] = b[0, x, y].astype(jnp.float32)
            raw[x, y, slots] = jnp.zeros((orb, orb), raw.dtype)
    load_blocks.wait()

    @pl.loop(0, tiles_x)
    def _(x):
        for t in range(2):
            codes = [code_ref[x, t, j] for j in range(slots)]
            live = count_ref[x, t]

            def block(code):
                slot = jnp.int32(0)
                for j in range(1, slots):
                    slot = jnp.where(codes[j] == code, j, slot)
                return raw[x, t, jnp.where(slot < live, slot, slots)]

            for shift in range(3):
                for s in range(2):
                    code = 3 * shift + s - t + 1
                    wx[
                        x,
                        shift * pair + s * orb : shift * pair + (s + 1) * orb,
                        t * orb : (t + 1) * orb,
                    ] = jnp.zeros((orb, orb), wx.dtype) if code in (2, 6) else block(code)
            for s, code in enumerate(((0, 3), (5, 8))[t]):
                wy[x, t, s * orb : (s + 1) * orb, :] = block(code)

    @pl.loop(0, groups)
    def _(g):
        interior(0, g)

    pl.semaphore_wait(barrier, 7 + line_n - 1 + plane_n - 1)

    @pl.loop(0, groups)
    def _(g):
        for copy in messages(0, g):
            copy.start()

    def to_sibling():
        return pltpu.make_async_remote_copy(
            src_ref=ga.at[core], dst_ref=ga.at[core], send_sem=ga_sem.at[0], recv_sem=ga_sem.at[1],
            device_id=sibling, device_id_type=MESH,
        )

    def to_plane(p, slot):
        return pltpu.make_async_remote_copy(
            src_ref=gb.at[slot], dst_ref=gb.at[slot],
            send_sem=gb_send.at[p], recv_sem=gb_recv.at[slot],
            device_id=plane_peer(p), device_id_type=MESH,
        )

    def to_line(p, slot):
        return pltpu.make_async_remote_copy(
            src_ref=gc.at[slot], dst_ref=gc.at[slot],
            send_sem=gc_send.at[p], recv_sem=gc_recv.at[slot],
            device_id=line_peer(p), device_id_type=MESH,
        )

    @pl.loop(0, ITERS * groups)
    def _(i):
        k, g = lax.div(i, groups), lax.rem(i, groups)
        r = rows_of(g)
        incoming = messages(k, g)
        incoming[4].wait_recv()
        incoming[5].wait_recv()
        for x in range(1, last):
            finish(k, g, x, acc[g, x] + jnp.concatenate([rim(k, g, x, 0), rim(k, g, x, 1)], axis=1))
        acc[g, 0, :, orb:] += rim(k, g, 0, 1)
        acc[g, last, :, :orb] += rim(k, g, last, 0)
        for m in range(4):
            incoming[m].wait_recv()
        acc[g, 0, :, :orb] += rim(k, g, 0, 0)
        acc[g, last, :, orb:] += rim(k, g, last, 1)
        for x, side, low in ((0, 0, 0), (last, 1, 2 * pair)):
            left = jnp.concatenate([xh[k, side, y, r, :] for y in range(2)], axis=1)
            image = acc[g, x] + jnp.dot(
                left, wx[x, low : low + pair, :], preferred_element_type=jnp.float32
            )
            finish(k, g, x, image)

        @pl.when(k < ITERS - 1)
        def _():
            for copy in messages(k + 1, g):
                copy.start()
            interior(k + 1, g)

        @pl.when(k == ITERS - 1)
        def _():
            pltpu.make_async_copy(
                b.at[ITERS, :, :, r], last_ref.at[:, :, r], out_sem.at[g]
            ).start()

        @pl.when(k == 1)
        def _():
            for s, (one, two) in enumerate(((1, 1), (1, 2), (1, 3), (2, 3), (3, 3))):
                product = sum(v[one, x, r, :] * v[two, x, r, :] for x in range(tiles_x))
                part[s, r, :] = product[:, :orb] + product[:, orb:]

        @pl.when(i == 2 * groups - 1)
        def _():
            ga[core] = jnp.zeros(ga.shape[1:], ga.dtype)
            for s in range(5):
                ga[core, s : s + 1, :] = jnp.sum(part[s].T, axis=0, keepdims=True)
            to_sibling().start()

        @pl.when(i == 2 * groups)
        def _():
            to_sibling().wait_recv()
            gb[my_plane] = ga[0] + ga[1]

            @pl.loop(1, plane_n)
            def _(j):
                to_plane(lax.rem(my_plane + j, plane_n), my_plane).start()

        @pl.when(i == 3 * groups - 1)
        def _():
            @pl.loop(1, plane_n)
            def _(j):
                p = lax.rem(my_plane + j, plane_n)
                to_plane(p, p).wait_recv()

            gc[my_line] = jnp.sum(gb[...], axis=0)

            @pl.loop(1, line_n)
            def _(j):
                to_line(lax.rem(my_line + j, line_n), my_line).start()

    @pl.loop(1, line_n)
    def _(j):
        p = lax.rem(my_line + j, line_n)
        to_line(p, p).wait_recv()

    sums = jnp.sum(gc[...], axis=0) / total_rows
    moments_ref[0:3, :] = sums[0:3]
    moments_ref[3:4, :] = 2.0 * sums[3:4] - sums[1:2]
    moments_ref[4:5, :] = 2.0 * sums[4:5] - sums[0:1]

    @pl.loop(0, ITERS * groups)
    def _(i):
        for copy in messages(lax.div(i, groups), lax.rem(i, groups)):
            copy.wait_send()

    to_sibling().wait_send()

    @pl.loop(1, plane_n)
    def _(j):
        to_plane(lax.rem(my_plane + j, plane_n), my_plane).wait_send()

    @pl.loop(1, line_n)
    def _(j):
        to_line(lax.rem(my_line + j, line_n), my_line).wait_send()

    for g in range(groups):
        r = pl.ds(g * rows, rows)
        pltpu.make_async_copy(b.at[ITERS, :, :, r], last_ref.at[:, :, r], out_sem.at[g]).wait()


def on_device(start_vectors, blocks, neighbour, counts):
    gx_n, gy_n = lax.axis_size("gx"), lax.axis_size("gy")
    tiles_x, tiles_y, vectors, orb = start_vectors.shape
    slots = neighbour.shape[2]
    groups, rows = GROUPS, vectors // GROUPS
    plane_n, line_n = gx_n // Z_HALVES, Z_HALVES * gy_n // CORES
    total_rows = tiles_x * gx_n * tiles_y * gy_n * orb
    assert tiles_y == 2 and tiles_x >= 3
    half, full = jnp.bfloat16, jnp.float32
    dma = pltpu.SemaphoreType.DMA
    return pl.pallas_call(
        functools.partial(kernel, gx_n, gy_n, groups, total_rows),
        out_shape=(
            jax.ShapeDtypeStruct((5, vectors), full),
            jax.ShapeDtypeStruct(start_vectors.shape, half),
        ),
        in_specs=[
            pl.BlockSpec(memory_space=pltpu.HBM),
            pl.BlockSpec(memory_space=pltpu.HBM),
            pl.BlockSpec(memory_space=pltpu.SMEM),
            pl.BlockSpec(memory_space=pltpu.SMEM),
        ],
        out_specs=(
            pl.BlockSpec(memory_space=pltpu.VMEM),
            pl.BlockSpec(memory_space=pltpu.HBM),
        ),
        scratch_shapes=[
            pltpu.VMEM((tiles_x, 2, slots + 1, orb, orb), half),
            pltpu.VMEM((tiles_x, 6 * orb, 2 * orb), half),
            pltpu.VMEM((tiles_x, 2, 2 * orb, orb), half),
            pltpu.VMEM((ITERS + 1, tiles_x, 2, vectors, orb), half),
            pltpu.VMEM((ITERS + 2, tiles_x, vectors, 2 * orb), full),
            pltpu.VMEM((groups, tiles_x, rows, 2 * orb), full),
            pltpu.VMEM((ITERS, 2, 2, vectors, orb), half),
            pltpu.VMEM((ITERS, 2, tiles_x + 1, vectors, orb), half),
            pltpu.VMEM((5, vectors, orb), full),
            pltpu.VMEM((2, 8, vectors), full),
            pltpu.VMEM((plane_n, 8, vectors), full),
            pltpu.VMEM((line_n, 8, vectors), full),
            dma((2,)),
            dma((groups,)),
            dma((ITERS * groups, 6)),
            dma((ITERS * groups, 6)),
            dma((2,)),
            dma((plane_n,)),
            dma((plane_n,)),
            dma((line_n,)),
            dma((line_n,)),
        ],
        compiler_params=pltpu.CompilerParams(
            collective_id=0, has_side_effects=True, vmem_limit_bytes=40 * 1024 * 1024
        ),
    )(start_vectors, blocks, neighbour, counts)


def solution(mesh):
    in_specs = (
        P("gx", "gy", None, None),
        P("gx", "gy", None, None, None),
        P("gx", "gy", None),
        P("gx", "gy"),
    )
    out_specs = (P(), P("gx", "gy", None, None))
    return jax.shard_map(
        on_device, mesh=mesh, in_specs=in_specs, out_specs=out_specs, check_vma=False
    )
```

```python
import functools

import jax
import jax.numpy as jnp
from jax import lax
from jax.experimental import pallas as pl
from jax.experimental.pallas import tpu as pltpu
from jax.sharding import PartitionSpec as P

ITERS = 4
GROUPS = 1
Y_SIZE = 4
Z_HALVES = 2
CORES = 2
MESH = pl.DeviceIdType.MESH


def kernel(
    gx_n, gy_n, groups, total_rows,
    start_ref, blocks_ref, code_ref, count_ref,
    moments_ref, last_ref,
    raw, wx, wy, wg, b, v, acc, xh, yh, ts, tg, part, ga, gb, gc,
    load_sem, out_sem, send_sem, recv_sem, block_sem, ga_sem, gb_send, gb_recv, gc_send, gc_recv,
):
    tiles_x, tiles_y, slots = code_ref.shape
    vectors, orb = start_ref.shape[2:]
    rows = vectors // groups
    pair = 2 * orb
    last = tiles_x - 1

    gx, gy = lax.axis_index("gx"), lax.axis_index("gy")
    east, west = lax.rem(gx + 1, gx_n), lax.rem(gx + gx_n - 1, gx_n)
    north, south = lax.rem(gy + 1, gy_n), lax.rem(gy + gy_n - 1, gy_n)

    x_size = gx_n // (Y_SIZE * Z_HALVES)
    z_lows = gy_n // CORES
    px = lax.div(gx, Y_SIZE * Z_HALVES)
    z_high = lax.rem(lax.div(gx, Y_SIZE), Z_HALVES)
    py = lax.rem(gx, Y_SIZE)
    z_low, core = lax.div(gy, CORES), lax.rem(gy, CORES)
    plane_n, line_n = x_size * Y_SIZE, Z_HALVES * z_lows
    my_plane, my_line = px * Y_SIZE + py, z_high * z_lows + z_low
    sibling = (gx, z_low * CORES + 1 - core)

    def plane_peer(p):
        peer_x, peer_y = lax.div(p, Y_SIZE), lax.rem(p, Y_SIZE)
        return (peer_x * (Y_SIZE * Z_HALVES) + z_high * Y_SIZE + peer_y, gy)

    def line_peer(p):
        high, low = lax.div(p, z_lows), lax.rem(p, z_lows)
        return (px * (Y_SIZE * Z_HALVES) + high * Y_SIZE + py, low * CORES + core)

    barrier = pltpu.get_barrier_semaphore()

    def greet(device):
        pl.semaphore_signal(barrier, inc=1, device_id=device, device_id_type=MESH)

    for device in (
        (east, gy), (west, gy), (east, north), (west, south), (gx, north), (gx, south), sibling,
    ):
        greet(device)

    @pl.loop(1, line_n)
    def _(j):
        greet(line_peer(lax.rem(my_line + j, line_n)))

    @pl.loop(1, plane_n)
    def _(j):
        greet(plane_peer(lax.rem(my_plane + j, plane_n)))

    load_start = pltpu.make_async_copy(start_ref, b.at[0], load_sem.at[0])
    load_blocks = pltpu.make_async_copy(
        blocks_ref, raw.at[:, :, pl.ds(0, slots)], load_sem.at[1]
    )
    load_blocks.start()
    load_start.start()

    def rows_of(g):
        return pl.ds(pl.multiple_of(g * rows, rows), rows)

    def messages(m, g, first=0, stop=12):
        k, r = 2 * m, rows_of(g)

        def along_y(level):
            return (
                (b.at[level, :, 1, r], yh.at[level, 0, pl.ds(1, tiles_x), r], (gx, north)),
                (b.at[level, :, 0, r], yh.at[level, 1, pl.ds(0, tiles_x), r], (gx, south)),
            )

        ends = (
            (b.at[k, last, :, r], xh.at[k, 0, :, r], (east, gy)),
            (b.at[k, 0, :, r], xh.at[k, 1, :, r], (west, gy)),
            (b.at[k, last, 1, r], yh.at[k, 0, 0, r], (east, north)),
            (b.at[k, 0, 0, r], yh.at[k, 1, tiles_x, r], (west, south)),
            *along_y(k),
            (ts.at[m, 1, :, r], tg.at[m, 0, pl.ds(1, 2), r], (east, gy)),
            (ts.at[m, 0, :, r], tg.at[m, 1, pl.ds(0, 2), r], (west, gy)),
            (ts.at[m, 1, 1, r], tg.at[m, 0, 0, r], (east, north)),
            (ts.at[m, 0, 0, r], tg.at[m, 1, 2, r], (west, south)),
            *along_y(k + 1),
        )
        return [
            pltpu.make_async_remote_copy(
                src_ref=source,
                dst_ref=target,
                send_sem=send_sem.at[m * groups + g, n],
                recv_sem=recv_sem.at[m * groups + g, n],
                device_id=device,
                device_id_type=MESH,
            )
            for n, (source, target, device) in enumerate(ends)
            if first <= n < stop
        ]

    def from_corner(m, g, n):
        return messages(m, g, n, n + 1)[0]

    def send(m, g, n):
        for copy in messages(m, g, n, n + 2):
            copy.start()
        if n in (0, 6):
            @pl.when(gy == gy_n - 1)
            def _():
                from_corner(m, g, n + 2).start()

            @pl.when(gy == 0)
            def _():
                from_corner(m, g, n + 3).start()

    def pass_on(m, g, n):
        k, r = 2 * m, rows_of(g)
        for copy in messages(m, g, n, n + 2):
            copy.wait_recv()
        if n == 0:
            ends = (
                (xh.at[k, 0, 1, r], yh.at[k, 0, 0, r], north, gy < gy_n - 1),
                (xh.at[k, 1, 0, r], yh.at[k, 1, tiles_x, r], south, gy > 0),
            )
        else:
            ends = (
                (tg.at[m, 0, 2, r], tg.at[m, 0, 0, r], north, gy < gy_n - 1),
                (tg.at[m, 1, 0, r], tg.at[m, 1, 2, r], south, gy > 0),
            )
        for side, (source, target, row, allowed) in enumerate(ends):
            copy = pltpu.make_async_remote_copy(
                src_ref=source,
                dst_ref=target,
                send_sem=send_sem.at[m * groups + g, n + 2 + side],
                recv_sem=recv_sem.at[m * groups + g, n + 2 + side],
                device_id=(gx, row),
                device_id_type=MESH,
            )
            pl.when(allowed)(copy.start)

    def wait_for(m, g, first, stop):
        for copy in messages(m, g, first, stop):
            copy.wait_recv()

    def block_messages():
        ends = (
            (wg.at[:, 2, pl.ds(0, orb)], wg.at[:, 0, pl.ds(0, orb)], (gx, north)),
            (wg.at[:, 0, pl.ds(orb, orb)], wg.at[:, 2, pl.ds(orb, orb)], (gx, south)),
        )
        return [
            pltpu.make_async_remote_copy(
                src_ref=source,
                dst_ref=target,
                send_sem=block_sem.at[0, n],
                recv_sem=block_sem.at[1, n],
                device_id=device,
                device_id_type=MESH,
            )
            for n, (source, target, device) in enumerate(ends)
        ]

    def interior(k, g):
        r = rows_of(g)
        for x in range(tiles_x):
            low, high = max(x - 1, 0), min(x + 1, last)
            left = jnp.concatenate(
                [b[k, s, y, r, :] for s in range(low, high + 1) for y in range(2)], axis=1
            )
            right = wx[x, (low - x + 1) * pair : (high - x + 2) * pair, :]
            acc[g, x] = jnp.dot(left, right, preferred_element_type=jnp.float32)

    def rim(k, g, x, side):
        r = rows_of(g)
        left = jnp.concatenate([yh[k, side, x, r, :], yh[k, side, x + 1, r, :]], axis=1)
        return jnp.dot(left, wy[x, side], preferred_element_type=jnp.float32)

    def scale(k):
        return jnp.where(k == 0, 1.0, 2.0)

    def corner(k, g, side):
        tile, x, low = ((0, 0, 0), (tiles_x, last, orb))[side]
        return jnp.dot(
            yh[k, side, tile, rows_of(g), :], wy[x, side, low : low + orb, :],
            preferred_element_type=jnp.float32,
        )

    def beside_corner(k, g, side):
        tile, x, low = ((1, 0, orb), (last, last, 0))[side]
        return jnp.dot(
            yh[k, side, tile, rows_of(g), :], wy[x, side, low : low + orb, :],
            preferred_element_type=jnp.float32,
        )

    def across(k, g, side):
        x, low = ((0, 0), (last, 2 * pair))[side]
        left = jnp.concatenate([xh[k, side, y, rows_of(g), :] for y in range(2)], axis=1)
        return jnp.dot(left, wx[x, low : low + pair, :], preferred_element_type=jnp.float32)

    def ghosts(m, g, corners):
        k, r = 2 * m, rows_of(g)
        for side, x in ((0, 0), (1, last)):
            column = [yh[k, 0, x + 1, r, :], b[k, x, 0, r, :], b[k, x, 1, r, :], yh[k, 1, x, r, :]]
            for q in range(3):
                if (q == 2 * side) != corners:
                    continue
                own = jnp.dot(
                    jnp.concatenate(column[q : q + 2], axis=1), wg[side, q],
                    preferred_element_type=jnp.float32,
                )
                value = tg[m, side, q, r, :].astype(jnp.float32) + scale(k) * own
                rounded = value.astype(jnp.bfloat16)
                if q == 2 * side:
                    yh[k + 1, side, side * tiles_x, r, :] = rounded
                else:
                    xh[k + 1, side, q - 1 + side, r, :] = rounded

    def finish(k, g, x, image):
        r = rows_of(g)
        value = scale(k) * image - v[k, x, r, :]
        v[k + 2, x, r, :] = value
        rounded = value.astype(jnp.bfloat16)
        for y in range(2):
            b[k + 1, x, y, r, :] = rounded[:, y * orb : (y + 1) * orb]

    load_start.wait()
    v[0] = jnp.zeros(v.shape[1:], v.dtype)
    for x in range(tiles_x):
        for y in range(2):
            v[1, x, :, y * orb : (y + 1) * orb] = b[0, x, y].astype(jnp.float32)
            raw[x, y, slots] = jnp.zeros((orb, orb), raw.dtype)
    load_blocks.wait()

    @pl.loop(0, tiles_x)
    def _(x):
        for t in range(2):
            codes = [code_ref[x, t, j] for j in range(slots)]
            live = count_ref[t, x]

            def block(code):
                slot = jnp.int32(0)
                for j in range(1, slots):
                    slot = jnp.where(codes[j] == code, j, slot)
                return raw[x, t, jnp.where(slot < live, slot, slots)]

            for shift in range(3):
                for s in range(2):
                    code = 3 * shift + s - t + 1
                    wx[
                        x,
                        shift * pair + s * orb : shift * pair + (s + 1) * orb,
                        t * orb : (t + 1) * orb,
                    ] = jnp.zeros((orb, orb), wx.dtype) if code in (2, 6) else block(code)
            for s, code in enumerate(((0, 3), (5, 8))[t]):
                wy[x, t, s * orb : (s + 1) * orb, :] = block(code)

    for t in range(2):
        row = slice(t * orb, (t + 1) * orb)
        wg[1, t, orb:, :] = wx[last, 2 * pair + t * orb : 2 * pair + (t + 1) * orb, row].T
        wg[0, t + 1, :orb, :] = wx[0, row, row].T
    wg[1, 1, :orb, :] = wx[last, 2 * pair + orb : 2 * pair + 2 * orb, :orb].T
    wg[1, 2, :orb, :] = wy[last, 1, orb:, :].T
    wg[0, 0, orb:, :] = wy[0, 0, :orb, :].T
    wg[0, 1, orb:, :] = wx[0, :orb, orb:].T

    @pl.loop(0, groups)
    def _(g):
        interior(0, g)

    pl.semaphore_wait(barrier, 7 + line_n - 1 + plane_n - 1)

    @pl.loop(0, groups)
    def _(g):
        send(0, g, 4)
        send(0, g, 0)

    for copy in block_messages():
        copy.start()

    def to_sibling():
        return pltpu.make_async_remote_copy(
            src_ref=ga.at[core], dst_ref=ga.at[core], send_sem=ga_sem.at[0], recv_sem=ga_sem.at[1],
            device_id=sibling, device_id_type=MESH,
        )

    def to_plane(p, slot):
        return pltpu.make_async_remote_copy(
            src_ref=gb.at[slot], dst_ref=gb.at[slot],
            send_sem=gb_send.at[p], recv_sem=gb_recv.at[slot],
            device_id=plane_peer(p), device_id_type=MESH,
        )

    def to_line(p, slot):
        return pltpu.make_async_remote_copy(
            src_ref=gc.at[slot], dst_ref=gc.at[slot],
            send_sem=gc_send.at[p], recv_sem=gc_recv.at[slot],
            device_id=line_peer(p), device_id_type=MESH,
        )

    @pl.loop(0, ITERS // 2)
    def _(m):
        k = 2 * m

        @pl.loop(0, groups)
        def _(g):
            r = rows_of(g)
            wait_for(m, g, 4, 6)
            acc[g, 0, :, :orb] += beside_corner(k, g, 0)
            acc[g, 0, :, orb:] += rim(k, g, 0, 1)
            acc[g, last, :, :orb] += rim(k, g, last, 0)
            acc[g, last, :, orb:] += beside_corner(k, g, 1)
            for side, x in ((1, last), (0, 0)):
                value = (scale(k) * acc[g, x] - v[k, x, r, :]).astype(jnp.bfloat16)
                for y in range(2):
                    ts[m, side, y, r, :] = value[:, y * orb : (y + 1) * orb]
            send(m, g, 6)
            for x in range(1, last):
                rims = jnp.concatenate([rim(k, g, x, 0), rim(k, g, x, 1)], axis=1)
                finish(k, g, x, acc[g, x] + rims)

        @pl.when(m == 1)
        def _():
            to_sibling().wait_recv()
            gb[my_plane] = ga[0] + ga[1]

            @pl.loop(1, plane_n)
            def _(j):
                to_plane(lax.rem(my_plane + j, plane_n), my_plane).start()

        @pl.loop(0, groups)
        def _(g):
            pass_on(m, g, 0)
            for side, x in ((1, last), (0, 0)):
                acc[g, x] += across(k, g, side)
            wait_for(m, g, 2, 4)
            acc[g, 0, :, :orb] += corner(k, g, 0)
            acc[g, last, :, orb:] += corner(k, g, 1)
            finish(k, g, last, acc[g, last])
            finish(k, g, 0, acc[g, 0])
            send(m, g, 10)
            interior(k + 1, g)

        @pl.when(m == 0)
        def _():
            for copy in block_messages():
                copy.wait_recv()

        @pl.when(m == 1)
        def _():
            @pl.loop(1, plane_n)
            def _(j):
                p = lax.rem(my_plane + j, plane_n)
                to_plane(p, p).wait_recv()

            gc[my_line] = jnp.sum(gb[...], axis=0)

            @pl.loop(1, line_n)
            def _(j):
                to_line(lax.rem(my_line + j, line_n), my_line).start()

        @pl.loop(0, groups)
        def _(g):
            r = rows_of(g)
            pass_on(m, g, 6)
            ghosts(m, g, False)
            wait_for(m, g, 8, 12)
            ghosts(m, g, True)
            for side, x in ((1, last), (0, 0)):
                rims = jnp.concatenate([rim(k + 1, g, x, 0), rim(k + 1, g, x, 1)], axis=1)
                finish(k + 1, g, x, acc[g, x] + rims + across(k + 1, g, side))

            @pl.when(m == 0)
            def _():
                send(1, g, 0)

            for x in range(1, last):
                rims = jnp.concatenate([rim(k + 1, g, x, 0), rim(k + 1, g, x, 1)], axis=1)
                finish(k + 1, g, x, acc[g, x] + rims)

            @pl.when(m == 0)
            def _():
                send(1, g, 4)
                interior(2, g)
                for s, (one, two) in enumerate(((1, 1), (1, 2), (1, 3), (2, 3), (3, 3))):
                    product = sum(v[one, x, r, :] * v[two, x, r, :] for x in range(tiles_x))
                    part[s, r, :] = product[:, :orb] + product[:, orb:]

            @pl.when(m == 1)
            def _():
                pltpu.make_async_copy(
                    b.at[ITERS, :, :, r], last_ref.at[:, :, r], out_sem.at[g]
                ).start()

        @pl.when(m == 0)
        def _():
            ga[core] = jnp.zeros(ga.shape[1:], ga.dtype)
            for s in range(5):
                ga[core, s : s + 1, :] = jnp.sum(part[s].T, axis=0, keepdims=True)
            to_sibling().start()

    @pl.loop(1, line_n)
    def _(j):
        p = lax.rem(my_line + j, line_n)
        to_line(p, p).wait_recv()

    sums = jnp.sum(gc[...], axis=0) / total_rows
    moments_ref[0:3, :] = sums[0:3]
    moments_ref[3:4, :] = 2.0 * sums[3:4] - sums[1:2]
    moments_ref[4:5, :] = 2.0 * sums[4:5] - sums[0:1]

    @pl.loop(0, ITERS // 2 * groups)
    def _(i):
        for copy in messages(lax.div(i, groups), lax.rem(i, groups)):
            copy.wait_send()

    for copy in block_messages():
        copy.wait_send()

    to_sibling().wait_send()

    @pl.loop(1, plane_n)
    def _(j):
        to_plane(lax.rem(my_plane + j, plane_n), my_plane).wait_send()

    @pl.loop(1, line_n)
    def _(j):
        to_line(lax.rem(my_line + j, line_n), my_line).wait_send()

    for g in range(groups):
        r = pl.ds(g * rows, rows)
        pltpu.make_async_copy(b.at[ITERS, :, :, r], last_ref.at[:, :, r], out_sem.at[g]).wait()


def on_device(start_vectors, blocks, neighbour, counts):
    gx_n, gy_n = lax.axis_size("gx"), lax.axis_size("gy")
    tiles_x, tiles_y, vectors, orb = start_vectors.shape
    slots = neighbour.shape[2]
    groups, rows = GROUPS, vectors // GROUPS
    plane_n, line_n = gx_n // Z_HALVES, Z_HALVES * gy_n // CORES
    total_rows = tiles_x * gx_n * tiles_y * gy_n * orb
    assert tiles_y == 2 and tiles_x >= 3
    half, full = jnp.bfloat16, jnp.float32
    dma = pltpu.SemaphoreType.DMA
    return pl.pallas_call(
        functools.partial(kernel, gx_n, gy_n, groups, total_rows),
        out_shape=(
            jax.ShapeDtypeStruct((5, vectors), full),
            jax.ShapeDtypeStruct(start_vectors.shape, half),
        ),
        in_specs=[
            pl.BlockSpec(memory_space=pltpu.HBM),
            pl.BlockSpec(memory_space=pltpu.HBM),
            pl.BlockSpec(memory_space=pltpu.SMEM),
            pl.BlockSpec(memory_space=pltpu.SMEM),
        ],
        out_specs=(
            pl.BlockSpec(memory_space=pltpu.VMEM),
            pl.BlockSpec(memory_space=pltpu.HBM),
        ),
        scratch_shapes=[
            pltpu.VMEM((tiles_x, 2, slots + 1, orb, orb), half),
            pltpu.VMEM((tiles_x, 6 * orb, 2 * orb), half),
            pltpu.VMEM((tiles_x, 2, 2 * orb, orb), half),
            pltpu.VMEM((2, 3, 2 * orb, orb), half),
            pltpu.VMEM((ITERS + 1, tiles_x, 2, vectors, orb), half),
            pltpu.VMEM((ITERS + 2, tiles_x, vectors, 2 * orb), full),
            pltpu.VMEM((groups, tiles_x, rows, 2 * orb), full),
            pltpu.VMEM((ITERS, 2, 2, vectors, orb), half),
            pltpu.VMEM((ITERS, 2, tiles_x + 1, vectors, orb), half),
            pltpu.VMEM((ITERS // 2, 2, 2, vectors, orb), half),
            pltpu.VMEM((ITERS // 2, 2, 3, vectors, orb), half),
            pltpu.VMEM((5, vectors, orb), full),
            pltpu.VMEM((2, 8, vectors), full),
            pltpu.VMEM((plane_n, 8, vectors), full),
            pltpu.VMEM((line_n, 8, vectors), full),
            dma((2,)),
            dma((groups,)),
            dma((ITERS // 2 * groups, 12)),
            dma((ITERS // 2 * groups, 12)),
            dma((2, 2)),
            dma((2,)),
            dma((plane_n,)),
            dma((plane_n,)),
            dma((line_n,)),
            dma((line_n,)),
        ],
        compiler_params=pltpu.CompilerParams(
            collective_id=0, has_side_effects=True, vmem_limit_bytes=54784 * 1024
        ),
    )(start_vectors, blocks, neighbour, counts.T)


def solution(mesh):
    in_specs = (
        P("gx", "gy", None, None),
        P("gx", "gy", None, None, None),
        P("gx", "gy", None),
        P("gx", "gy"),
    )
    out_specs = (P(), P("gx", "gy", None, None))
    return jax.shard_map(
        on_device, mesh=mesh, in_specs=in_specs, out_specs=out_specs, check_vma=False
    )
```

```python
import functools

import jax
import jax.numpy as jnp
from jax import lax
from jax.experimental import pallas as pl
from jax.experimental.pallas import tpu as pltpu
from jax.sharding import PartitionSpec as P

ITERS = 4
GROUPS = 1
Y_SIZE = 4
Z_HALVES = 2
CORES = 2
FIRST = 0
MESH = pl.DeviceIdType.MESH


def kernel(
    gx_n, gy_n, groups, total_rows,
    start_ref, blocks_ref, code_ref, count_ref,
    moments_ref, last_ref,
    raw, wx, wy, wg, b, v, acc, xh, yh, ts, tg, ga, gb, gc,
    load_sem, out_sem, send_sem, recv_sem, block_sem, ga_sem, gb_send, gb_recv, gc_send, gc_recv,
):
    tiles_x, tiles_y, slots = code_ref.shape
    vectors, orb = start_ref.shape[2:]
    rows = vectors // groups
    pair = 2 * orb
    last = tiles_x - 1

    gx, gy = lax.axis_index("gx"), lax.axis_index("gy")
    east, west = lax.rem(gx + 1, gx_n), lax.rem(gx + gx_n - 1, gx_n)
    north, south = lax.rem(gy + 1, gy_n), lax.rem(gy + gy_n - 1, gy_n)

    x_size = gx_n // (Y_SIZE * Z_HALVES)
    z_lows = gy_n // CORES
    px = lax.div(gx, Y_SIZE * Z_HALVES)
    z_high = lax.rem(lax.div(gx, Y_SIZE), Z_HALVES)
    py = lax.rem(gx, Y_SIZE)
    z_low, core = lax.div(gy, CORES), lax.rem(gy, CORES)
    plane_n, line_n = x_size * Y_SIZE, Z_HALVES * z_lows
    my_plane, my_line = px * Y_SIZE + py, z_high * z_lows + z_low
    sibling = (gx, z_low * CORES + 1 - core)

    def plane_peer(p):
        peer_x, peer_y = lax.div(p, Y_SIZE), lax.rem(p, Y_SIZE)
        return (peer_x * (Y_SIZE * Z_HALVES) + z_high * Y_SIZE + peer_y, gy)

    def line_peer(p):
        high, low = lax.div(p, z_lows), lax.rem(p, z_lows)
        return (px * (Y_SIZE * Z_HALVES) + high * Y_SIZE + py, low * CORES + core)

    barrier = pltpu.get_barrier_semaphore()

    def greet(device):
        pl.semaphore_signal(barrier, inc=1, device_id=device, device_id_type=MESH)

    for device in (
        (east, gy), (west, gy), (east, north), (west, south), (gx, north), (gx, south), sibling,
    ):
        greet(device)

    @pl.loop(1, line_n)
    def _(j):
        greet(line_peer(lax.rem(my_line + j, line_n)))

    @pl.loop(1, plane_n)
    def _(j):
        greet(plane_peer(lax.rem(my_plane + j, plane_n)))

    load_start = pltpu.make_async_copy(start_ref, b.at[0], load_sem.at[0])
    load_blocks = pltpu.make_async_copy(
        blocks_ref, raw.at[:, :, pl.ds(0, slots)], load_sem.at[1]
    )
    load_blocks.start()
    load_start.start()

    def rows_of(g):
        return pl.ds(pl.multiple_of(g * rows, rows), rows)

    def messages(m, g, first=0, stop=12):
        k, r = 2 * m, rows_of(g)

        def along_y(level):
            return (
                (b.at[level, :, 1, r], yh.at[level, 0, pl.ds(1, tiles_x), r], (gx, north)),
                (b.at[level, :, 0, r], yh.at[level, 1, pl.ds(0, tiles_x), r], (gx, south)),
            )

        ends = (
            (b.at[k, last, :, r], xh.at[k, 0, :, r], (east, gy)),
            (b.at[k, 0, :, r], xh.at[k, 1, :, r], (west, gy)),
            (b.at[k, last, 1, r], yh.at[k, 0, 0, r], (east, north)),
            (b.at[k, 0, 0, r], yh.at[k, 1, tiles_x, r], (west, south)),
            *along_y(k),
            (ts.at[m, 1, :, r], tg.at[m, 0, pl.ds(1, 2), r], (east, gy)),
            (ts.at[m, 0, :, r], tg.at[m, 1, pl.ds(0, 2), r], (west, gy)),
            (ts.at[m, 1, 1, r], tg.at[m, 0, 0, r], (east, north)),
            (ts.at[m, 0, 0, r], tg.at[m, 1, 2, r], (west, south)),
            *along_y(k + 1),
        )
        return [
            pltpu.make_async_remote_copy(
                src_ref=source,
                dst_ref=target,
                send_sem=send_sem.at[m * groups + g, n],
                recv_sem=recv_sem.at[m * groups + g, n],
                device_id=device,
                device_id_type=MESH,
            )
            for n, (source, target, device) in enumerate(ends)
            if first <= n < stop
        ]

    def from_corner(m, g, n):
        return messages(m, g, n, n + 1)[0]

    def halves(m, g, n):
        k = 2 * m
        out = []
        for y in range(2):
            ends = (
                ((b.at[k, last, y], xh.at[k, 0, y], east, 0), (b.at[k, 0, y], xh.at[k, 1, y], west, 1))
                if n == 0
                else ((ts.at[m, 1, y], tg.at[m, 0, 1 + y], east, 0), (ts.at[m, 0, y], tg.at[m, 1, y], west, 1))
            )
            for source, target, column, side in ends:
                out.append(pltpu.make_async_remote_copy(
                    src_ref=source, dst_ref=target,
                    send_sem=send_sem.at[m * groups + g, n + side],
                    recv_sem=recv_sem.at[m * groups + g, n + side],
                    device_id=(column, gy), device_id_type=MESH))
        return out

    def send(m, g, n):
        for copy in (messages(m, g, n, n + 2) if n not in (0, 6) else halves(m, g, n)):
            copy.start()
        if n in (0, 6):
            @pl.when(gy == gy_n - 1)
            def _():
                from_corner(m, g, n + 2).start()

            @pl.when(gy == 0)
            def _():
                from_corner(m, g, n + 3).start()

    def pass_on(m, g, n):
        k, r = 2 * m, rows_of(g)
        for copy in messages(m, g, n, n + 2):
            copy.wait_recv()
        if n == 0:
            ends = (
                (xh.at[k, 0, 1, r], yh.at[k, 0, 0, r], north, gy < gy_n - 1),
                (xh.at[k, 1, 0, r], yh.at[k, 1, tiles_x, r], south, gy > 0),
            )
        else:
            ends = (
                (tg.at[m, 0, 2, r], tg.at[m, 0, 0, r], north, gy < gy_n - 1),
                (tg.at[m, 1, 0, r], tg.at[m, 1, 2, r], south, gy > 0),
            )
        for side, (source, target, row, allowed) in enumerate(ends):
            copy = pltpu.make_async_remote_copy(
                src_ref=source,
                dst_ref=target,
                send_sem=send_sem.at[m * groups + g, n + 2 + side],
                recv_sem=recv_sem.at[m * groups + g, n + 2 + side],
                device_id=(gx, row),
                device_id_type=MESH,
            )
            pl.when(allowed)(copy.start)

    def wait_for(m, g, first, stop):
        for copy in messages(m, g, first, stop):
            copy.wait_recv()

    def block_messages():
        ends = (
            (wg.at[:, 2, pl.ds(0, orb)], wg.at[:, 0, pl.ds(0, orb)], (gx, north)),
            (wg.at[:, 0, pl.ds(orb, orb)], wg.at[:, 2, pl.ds(orb, orb)], (gx, south)),
        )
        return [
            pltpu.make_async_remote_copy(
                src_ref=source,
                dst_ref=target,
                send_sem=block_sem.at[0, n],
                recv_sem=block_sem.at[1, n],
                device_id=device,
                device_id_type=MESH,
            )
            for n, (source, target, device) in enumerate(ends)
        ]

    def interior(k, g, columns):
        r = rows_of(g)
        for x in columns:
            low, high = max(x - 1, 0), min(x + 1, last)
            left = jnp.concatenate(
                [b[k, s, y, r, :] for s in range(low, high + 1) for y in range(2)], axis=1
            )
            right = wx[x, (low - x + 1) * pair : (high - x + 2) * pair, :]
            acc[g, x] = jnp.dot(left, right, preferred_element_type=jnp.float32)

    def rim(k, g, x, side):
        r = rows_of(g)
        left = jnp.concatenate([yh[k, side, x, r, :], yh[k, side, x + 1, r, :]], axis=1)
        return jnp.dot(left, wy[x, side], preferred_element_type=jnp.float32)

    def scale(k):
        return jnp.where(k == 0, 1.0, 2.0)

    def corner(k, g, side):
        tile, x, low = ((0, 0, 0), (tiles_x, last, orb))[side]
        return jnp.dot(
            yh[k, side, tile, rows_of(g), :], wy[x, side, low : low + orb, :],
            preferred_element_type=jnp.float32,
        )

    def beside_corner(k, g, side):
        tile, x, low = ((1, 0, orb), (last, last, 0))[side]
        return jnp.dot(
            yh[k, side, tile, rows_of(g), :], wy[x, side, low : low + orb, :],
            preferred_element_type=jnp.float32,
        )

    def across(k, g, side):
        x, low = ((0, 0), (last, 2 * pair))[side]
        left = jnp.concatenate([xh[k, side, y, rows_of(g), :] for y in range(2)], axis=1)
        return jnp.dot(left, wx[x, low : low + pair, :], preferred_element_type=jnp.float32)

    def ghosts(m, g, corners):
        k, r = 2 * m, rows_of(g)
        for side, x in ((0, 0), (1, last)):
            column = [yh[k, 0, x + 1, r, :], b[k, x, 0, r, :], b[k, x, 1, r, :], yh[k, 1, x, r, :]]
            for q in range(3):
                if (q == 2 * side) != corners:
                    continue
                own = jnp.dot(
                    jnp.concatenate(column[q : q + 2], axis=1), wg[side, q],
                    preferred_element_type=jnp.float32,
                )
                value = tg[m, side, q, r, :].astype(jnp.float32) + scale(k) * own
                rounded = value.astype(jnp.bfloat16)
                if q == 2 * side:
                    yh[k + 1, side, side * tiles_x, r, :] = rounded
                else:
                    xh[k + 1, side, q - 1 + side, r, :] = rounded

    def finish(k, g, x, image):
        r = rows_of(g)
        value = scale(k) * image - v[k, x, r, :]
        v[k + 2, x, r, :] = value
        rounded = value.astype(jnp.bfloat16)
        for y in range(2):
            b[k + 1, x, y, r, :] = rounded[:, y * orb : (y + 1) * orb]

    load_start.wait()
    v[0] = jnp.zeros(v.shape[1:], v.dtype)
    for x in range(tiles_x):
        for y in range(2):
            v[1, x, :, y * orb : (y + 1) * orb] = b[0, x, y].astype(jnp.float32)
            raw[x, y, slots] = jnp.zeros((orb, orb), raw.dtype)
    load_blocks.wait()

    @pl.loop(0, tiles_x)
    def _(x):
        for t in range(2):
            codes = [code_ref[x, t, j] for j in range(slots)]
            live = count_ref[t, x]

            def block(code):
                slot = jnp.int32(0)
                for j in range(1, slots):
                    slot = jnp.where(codes[j] == code, j, slot)
                return raw[x, t, jnp.where(slot < live, slot, slots)]

            for shift in range(3):
                for s in range(2):
                    code = 3 * shift + s - t + 1
                    wx[
                        x,
                        shift * pair + s * orb : shift * pair + (s + 1) * orb,
                        t * orb : (t + 1) * orb,
                    ] = jnp.zeros((orb, orb), wx.dtype) if code in (2, 6) else block(code)
            for s, code in enumerate(((0, 3), (5, 8))[t]):
                wy[x, t, s * orb : (s + 1) * orb, :] = block(code)

    for t in range(2):
        row = slice(t * orb, (t + 1) * orb)
        wg[1, t, orb:, :] = wx[last, 2 * pair + t * orb : 2 * pair + (t + 1) * orb, row].T
        wg[0, t + 1, :orb, :] = wx[0, row, row].T
    wg[1, 1, :orb, :] = wx[last, 2 * pair + orb : 2 * pair + 2 * orb, :orb].T
    wg[1, 2, :orb, :] = wy[last, 1, orb:, :].T
    wg[0, 0, orb:, :] = wy[0, 0, :orb, :].T
    wg[0, 1, orb:, :] = wx[0, :orb, orb:].T

    edges, inner = (0, last), range(1, last)

    @pl.loop(0, groups)
    def _(g):
        interior(0, g, edges)

    pl.semaphore_wait(barrier, 7 + line_n - 1 + plane_n - 1)

    @pl.loop(0, groups)
    def _(g):
        send(0, g, 4)
        send(0, g, 0)

    for copy in block_messages():
        copy.start()

    def to_sibling():
        return pltpu.make_async_remote_copy(
            src_ref=ga.at[core], dst_ref=ga.at[core], send_sem=ga_sem.at[0], recv_sem=ga_sem.at[1],
            device_id=sibling, device_id_type=MESH,
        )

    def to_plane(p, slot):
        return pltpu.make_async_remote_copy(
            src_ref=gb.at[slot], dst_ref=gb.at[slot],
            send_sem=gb_send.at[p], recv_sem=gb_recv.at[slot],
            device_id=plane_peer(p), device_id_type=MESH,
        )

    def to_line(p, slot):
        return pltpu.make_async_remote_copy(
            src_ref=gc.at[slot, pl.ds(0, 5)], dst_ref=gc.at[slot, pl.ds(0, 5)],
            send_sem=gc_send.at[p], recv_sem=gc_recv.at[slot],
            device_id=line_peer(p), device_id_type=MESH,
        )

    def add_rims(k, g):
        acc[g, 0, :, :orb] += beside_corner(k, g, 0)
        acc[g, 0, :, orb:] += rim(k, g, 0, 1)
        acc[g, last, :, :orb] += rim(k, g, last, 0)
        acc[g, last, :, orb:] += beside_corner(k, g, 1)

    def add_corners(k, g):
        acc[g, 0, :, :orb] += corner(k, g, 0)
        acc[g, last, :, orb:] += corner(k, g, 1)

    def middle(k, g):
        interior(k, g, inner)
        for x in inner:
            rims = jnp.concatenate([rim(k, g, x, 0), rim(k, g, x, 1)], axis=1)
            finish(k, g, x, acc[g, x] + rims)

    @pl.loop(0, ITERS // 2)
    def _(m):
        k = 2 * m

        @pl.loop(0, groups)
        def _(g):
            r = rows_of(g)
            wait_for(m, g, 4, 6)
            add_rims(k, g)
            for side, x in ((1, last), (0, 0)):
                value = (scale(k) * acc[g, x] - v[k, x, r, :]).astype(jnp.bfloat16)
                for y in range(2):
                    ts[m, side, y, r, :] = value[:, y * orb : (y + 1) * orb]
            send(m, g, 6)
            middle(k, g)

        @pl.when(m == 1)
        def _():
            ga[core] = jnp.zeros(ga.shape[1:], ga.dtype)
            for s, (one, two) in enumerate(((1, 1), (1, 2), (1, 3), (2, 3), (3, 3))):
                product = sum(v[one, x] * v[two, x] for x in range(tiles_x))
                product = product[:, :orb] + product[:, orb:]
                ga[core, s : s + 1, :] = jnp.sum(product.T, axis=0, keepdims=True)
            to_sibling().start()
            to_sibling().wait_recv()
            gb[my_plane] = ga[0] + ga[1]

            @pl.loop(1, plane_n)
            def _(j):
                to_plane(lax.rem(my_plane + j, plane_n), my_plane).start()

        @pl.loop(0, groups)
        def _(g):
            pass_on(m, g, 0)
            for side, x in ((1, last), (0, 0)):
                acc[g, x] += across(k, g, side)
            wait_for(m, g, 2, 4)
            add_corners(k, g)
            finish(k, g, last, acc[g, last])
            finish(k, g, 0, acc[g, 0])
            send(m, g, 10)
            interior(k + 1, g, edges)

        @pl.when(m == 0)
        def _():
            for copy in block_messages():
                copy.wait_recv()

        @pl.when(m == 1)
        def _():
            @pl.loop(1, plane_n)
            def _(j):
                p = lax.rem(my_plane + j, plane_n)
                to_plane(p, p).wait_recv()

            gc[my_line] = jnp.sum(gb[...], axis=0)

            @pl.loop(1, line_n)
            def _(j):
                to_line(lax.rem(my_line + j, line_n), my_line).start()

        @pl.loop(0, groups)
        def _(g):
            r = rows_of(g)
            pass_on(m, g, 6)
            ghosts(m, g, False)
            for side, x in ((1, last), (0, 0)):
                acc[g, x] += across(k + 1, g, side)
            wait_for(m, g, 10, 12)
            add_rims(k + 1, g)
            wait_for(m, g, 8, 10)
            ghosts(m, g, True)
            add_corners(k + 1, g)
            finish(k + 1, g, last, acc[g, last])
            finish(k + 1, g, 0, acc[g, 0])

            @pl.when(m == 0)
            def _():
                send(1, g, 0)

            middle(k + 1, g)

            @pl.when(m == 0)
            def _():
                send(1, g, 4)
                interior(2, g, edges)

            @pl.when(m == 1)
            def _():
                pltpu.make_async_copy(
                    b.at[ITERS, :, :, r], last_ref.at[:, :, r], out_sem.at[g]
                ).start()

    @pl.loop(1, line_n)
    def _(j):
        p = lax.rem(my_line + j, line_n)
        to_line(p, p).wait_recv()

    sums = jnp.sum(gc[:, 0:5, :], axis=0) / total_rows
    moments_ref[0:3, :] = sums[0:3]
    moments_ref[3:4, :] = 2.0 * sums[3:4] - sums[1:2]
    moments_ref[4:5, :] = 2.0 * sums[4:5] - sums[0:1]

    @pl.loop(0, ITERS // 2 * groups)
    def _(i):
        for copy in messages(lax.div(i, groups), lax.rem(i, groups)):
            copy.wait_send()

    for copy in block_messages():
        copy.wait_send()

    to_sibling().wait_send()

    @pl.loop(1, plane_n)
    def _(j):
        to_plane(lax.rem(my_plane + j, plane_n), my_plane).wait_send()

    @pl.loop(1, line_n)
    def _(j):
        to_line(lax.rem(my_line + j, line_n), my_line).wait_send()

    for g in range(groups):
        r = pl.ds(g * rows, rows)
        pltpu.make_async_copy(b.at[ITERS, :, :, r], last_ref.at[:, :, r], out_sem.at[g]).wait()


def on_device(start_vectors, blocks, neighbour, counts):
    gx_n, gy_n = lax.axis_size("gx"), lax.axis_size("gy")
    tiles_x, tiles_y, vectors, orb = start_vectors.shape
    slots = neighbour.shape[2]
    groups, rows = GROUPS, vectors // GROUPS
    plane_n, line_n = gx_n // Z_HALVES, Z_HALVES * gy_n // CORES
    total_rows = tiles_x * gx_n * tiles_y * gy_n * orb
    assert tiles_y == 2 and tiles_x >= 3
    half, full = jnp.bfloat16, jnp.float32
    dma = pltpu.SemaphoreType.DMA
    return pl.pallas_call(
        functools.partial(kernel, gx_n, gy_n, groups, total_rows),
        out_shape=(
            jax.ShapeDtypeStruct((5, vectors), full),
            jax.ShapeDtypeStruct(start_vectors.shape, half),
        ),
        in_specs=[
            pl.BlockSpec(memory_space=pltpu.HBM),
            pl.BlockSpec(memory_space=pltpu.HBM),
            pl.BlockSpec(memory_space=pltpu.SMEM),
            pl.BlockSpec(memory_space=pltpu.SMEM),
        ],
        out_specs=(
            pl.BlockSpec(memory_space=pltpu.VMEM),
            pl.BlockSpec(memory_space=pltpu.HBM),
        ),
        scratch_shapes=[
            pltpu.VMEM((tiles_x, 2, slots + 1, orb, orb), half),
            pltpu.VMEM((tiles_x, 6 * orb, 2 * orb), half),
            pltpu.VMEM((tiles_x, 2, 2 * orb, orb), half),
            pltpu.VMEM((2, 3, 2 * orb, orb), half),
            pltpu.VMEM((ITERS + 1, tiles_x, 2, vectors, orb), half),
            pltpu.VMEM((ITERS + 2, tiles_x, vectors, 2 * orb), full),
            pltpu.VMEM((groups, tiles_x, rows, 2 * orb), full),
            pltpu.VMEM((ITERS, 2, 2, vectors, orb), half),
            pltpu.VMEM((ITERS, 2, tiles_x + 1, vectors, orb), half),
            pltpu.VMEM((ITERS // 2, 2, 2, vectors, orb), half),
            pltpu.VMEM((ITERS // 2, 2, 3, vectors, orb), half),
            pltpu.VMEM((2, 8, vectors), full),
            pltpu.VMEM((plane_n, 8, vectors), full),
            pltpu.VMEM((line_n, 8, vectors), full),
            dma((2,)),
            dma((groups,)),
            dma((ITERS // 2 * groups, 12)),
            dma((ITERS // 2 * groups, 12)),
            dma((2, 2)),
            dma((2,)),
            dma((plane_n,)),
            dma((plane_n,)),
            dma((line_n,)),
            dma((line_n,)),
        ],
        compiler_params=pltpu.CompilerParams(
            collective_id=0, has_side_effects=True, vmem_limit_bytes=54784 * 1024
        ),
    )(start_vectors, blocks, neighbour, counts.T)


def solution(mesh):
    in_specs = (
        P("gx", "gy", None, None),
        P("gx", "gy", None, None, None),
        P("gx", "gy", None),
        P("gx", "gy"),
    )
    out_specs = (P(), P("gx", "gy", None, None))
    return jax.shard_map(
        on_device, mesh=mesh, in_specs=in_specs, out_specs=out_specs, check_vma=False
    )
```
